32 devices in a mesh: groups: 2 (over x), queue: 16 (over z, y, core).
Axes of the slice: x: 2, y: 2, z: 4, core: 2. Of those that a mesh axis runs over, the one named last changes fastest.
Arguments:
- query: bfloat16 [32, 768, 2560], P(('groups', 'queue')), parts along dimension 0, may hold values from -6 to 6
- keys: bfloat16 [32, 768, 2560], P(('groups', 'queue')), parts along dimension 0, may hold values from -6 to 6
- values: bfloat16 [32, 768, 2560], P(('groups', 'queue')), parts along dimension 0, may hold values from -6 to 6
- gate_table: float32 [50, 2, 2560], replicated, may hold values from 0.5 to 2
- levels: int32 [32], P('groups'), parts along dimension 0, may hold values from 0 to 49
- window: int32 [32], P('groups'), parts along dimension 0, may hold values from 0 to 2, as said below
- queue_head: int32 [2], P('groups'), parts along dimension 0, may hold values from 1 to 15
Outputs:
- attended: bfloat16 [32, 768, 2560], P(('groups', 'queue')), parts along dimension 0
The draws below stay inside these ranges and needn't reach their ends.
There are 2 independent parts, one for each index of `groups`. The reference program is written for one: setup_inputs(seed, part) draws one part's arguments, and reference() takes and returns one part's arrays. A program takes and returns all parts, laid end to end along the dimension named above; an argument that names none is the same for every part. Nothing has to cross between parts.
Inputs may be any that keep to these rules, and one draw needn't show every extreme that they name: `window`: at least one slot has width 2.
All inputs are finite; a program needn't handle non-finite values.
Results may differ from the reference program's by a relative error of at most 0.008.
Values may be sent and summed in bfloat16 or wider, within the bound.
A program may use at most 192 MiB of HBM per device.

```python
import math
import jax
import jax.numpy as jnp
from jax import lax

HEADS = 20
HEAD_DIM = 128
FRAME_TOK = 768
REACH = 2
LEVELS = 50
SLOTS = 16
D = 2560


def draw_pair(key, which):
    shape = (SLOTS, FRAME_TOK, HEADS, HEAD_DIM)
    result = jnp.clip(jax.random.normal(jax.random.fold_in(key, 3 + which), shape, jnp.float32), -6.0, 6.0)
    return result.reshape(SLOTS, FRAME_TOK, HEADS * HEAD_DIM).astype(jnp.bfloat16)


def draw_query(key, part):
    return draw_pair(key, 0)


def draw_keys(key, part):
    return draw_pair(key, 1)


def draw_window(key, part):
    drawn = jax.random.randint(jax.random.fold_in(key, 29), (SLOTS,), 0, REACH + 1)
    return jnp.where(jnp.arange(SLOTS) == 0, REACH, drawn).astype(jnp.int32)


def place_ends(values, stream_key, low, top_value):
    longest = values.shape.index(max(values.shape))
    spots = []
    for shift in (0, 1):
        where = [jax.random.randint(jax.random.fold_in(stream_key, axis), (), 0, length) for axis, length in enumerate(values.shape)]
        where[longest] = (where[longest] + shift) % values.shape[longest]
        spots.append(tuple(where))
    return values.at[spots[0]].set(low).at[spots[1]].set(top_value)


def block_levels(rng, shape, shards, smallest, largest):
    gain = 1.0
    for axis_at, shards_of in shards:
        draws = jax.random.uniform(jax.random.fold_in(jax.random.fold_in(rng, 6), axis_at), (shards_of,), jnp.float32, smallest / len(shards), largest / len(shards))
        gain = gain * jnp.repeat(jnp.exp(draws), shape[axis_at] // shards_of).reshape((-1,) + (1,) * (len(shape) - 1 - axis_at))
    return gain


def scatter_about(stream_key, extent, width, bound, shards=(), kind=jnp.bfloat16):
    values = width * jax.random.normal(stream_key, extent, jnp.float32)
    if shards:
        values = values * block_levels(stream_key, extent, shards, -0.22, 0.18)
    return jnp.clip(values, -bound, bound).astype(kind)


def setup_inputs(seed: int = 0, part: int = 0) -> dict:
    key_list = jax.random.split(jax.random.key(seed), 8)
    part_splits = jax.random.split(jax.random.fold_in(key_list[7], part), 8)
    query = draw_query(jax.random.fold_in(jax.random.fold_in(key_list[7], part), 71), part)
    keys = draw_keys(jax.random.fold_in(jax.random.fold_in(key_list[7], part), 71), part)
    values = scatter_about(part_splits[2], (SLOTS, FRAME_TOK, D), 1.0, 6.0, ((0, 16),))
    gate_table = jnp.clip(jnp.exp(jax.random.uniform(key_list[3], (LEVELS, 2, D), jnp.float32, math.log(0.5), math.log(2.0))), 0.5, 2.0)
    levels = place_ends(jax.random.randint(part_splits[4], (SLOTS,), 0, LEVELS), jax.random.fold_in(part_splits[4], 1), 0, LEVELS - 1).astype(jnp.int32)
    window = draw_window(jax.random.fold_in(jax.random.fold_in(key_list[7], part), 71), part)
    queue_head = jax.random.randint(part_splits[6], (1,), 1, SLOTS).astype(jnp.int32)
    return {"query": query, "keys": keys, "values": values, "gate_table": gate_table, "levels": levels, "window": window, "queue_head": queue_head}


def spatial_frame(query_f, keys_f, values_f):
    head_groups = math.gcd(HEADS, 4)
    per_group = HEADS // head_groups
    span_cols = per_group * HEAD_DIM
    score_scale = 1.0 / math.sqrt(HEAD_DIM)
    pieces = []
    for group_index in range(head_groups):
        lower = group_index * span_cols
        q_part = query_f[:, lower:lower + span_cols].reshape(FRAME_TOK, per_group, HEAD_DIM).astype(jnp.float32)
        k_part = keys_f[:, lower:lower + span_cols].reshape(FRAME_TOK, per_group, HEAD_DIM).astype(jnp.float32)
        v_part = values_f[:, lower:lower + span_cols].reshape(FRAME_TOK, per_group, HEAD_DIM).astype(jnp.float32)
        scores = jnp.einsum('qhd,khd->hqk', q_part, k_part) * score_scale
        top_score = lax.optimization_barrier(jnp.max(scores, axis=-1, keepdims=True))
        expd = jnp.exp(scores - top_score)
        weights = (expd / lax.optimization_barrier(jnp.sum(expd, axis=-1, keepdims=True))).astype(jnp.bfloat16)
        mixed_part = jnp.einsum('hqk,khd->qhd', weights.astype(jnp.float32), v_part)
        pieces.append(mixed_part.reshape(FRAME_TOK, span_cols))
    return jnp.concatenate(pieces, axis=1)

def reference(query, keys, values, gate_table, levels, window, queue_head):
    spatial = lax.map(lambda trio: spatial_frame(trio[0], trio[1], trio[2]), (query, keys, values))
    slot_count = query.shape[0]
    score_scale = 1.0 / math.sqrt(HEAD_DIM)
    positions = (jnp.arange(slot_count, dtype=jnp.int32) - queue_head[0]) % slot_count
    query_four = query.reshape(slot_count, FRAME_TOK, HEADS, HEAD_DIM).astype(jnp.float32)
    score_list = []
    value_list = []
    for offset in range(-REACH, REACH + 1):
        keys_near = jnp.roll(keys, -offset, axis=0).reshape(slot_count, FRAME_TOK, HEADS, HEAD_DIM).astype(jnp.float32)
        values_near = jnp.roll(values, -offset, axis=0).reshape(slot_count, FRAME_TOK, HEADS, HEAD_DIM)
        scores = jnp.einsum('sthd,sthd->sth', query_four, keys_near) * score_scale
        valid = (abs(offset) <= window) & (positions + offset >= 0) & (positions + offset < slot_count)
        score_list.append(jnp.where(valid[:, None, None], scores, -1e+30))
        value_list.append(values_near)
    stacked = jnp.stack(score_list)
    top_score = lax.optimization_barrier(jnp.max(stacked, axis=0))
    expd = jnp.exp(stacked - top_score[None])
    weights = expd / lax.optimization_barrier(jnp.sum(expd, axis=0))[None]
    temporal = jnp.zeros((slot_count, FRAME_TOK, HEADS, HEAD_DIM), jnp.float32)
    for index in range(len(value_list)):
        temporal = temporal + weights[index][..., None] * value_list[index].astype(jnp.float32)
    temporal = temporal.astype(jnp.bfloat16).reshape(slot_count, FRAME_TOK, D)
    gates = gate_table[levels]
    blended = gates[:, 0][:, None, :] * spatial + gates[:, 1][:, None, :] * temporal.astype(jnp.float32)
    return blended.astype(jnp.bfloat16)
```

```python
import functools
import math

import jax
import jax.numpy as jnp
from jax import lax
from jax.experimental import pallas as pl
from jax.experimental.pallas import tpu as pltpu
from jax.sharding import PartitionSpec as P

HEAD_DIM = 128
REACH = 2
TEAM = 4
CHUNK_HEADS = 2
ROW_BLOCK = 256
AHEAD = 2
LAG_TEMPORAL = 1
LAG_BLEND = 1
K, V, Q = 0, 1, 2


def kernel(
    n,
    levels_ref,
    window_ref,
    head_ref,
    gate_ref,
    q_hbm,
    k_hbm,
    v_hbm,
    out_hbm,
    own,
    swap,
    spatial,
    back,
    load_sem,
    swap_send,
    swap_recv,
    swap_local,
    halo_send,
    halo_recv,
    back_send,
    back_recv,
    back_local,
    out_sem,
):
    tokens, width = back.shape
    quarter = tokens // TEAM
    chunk = CHUNK_HEADS * HEAD_DIM
    count = width // chunk
    coef = math.log2(math.e) / math.sqrt(HEAD_DIM)

    slot = lax.axis_index("queue")
    place = lax.rem(slot, TEAM)
    team = slot - place
    following = lax.rem(slot + TEAM, n)
    previous = lax.rem(slot + n - TEAM, n)

    def cols(c):
        return pl.ds(pl.multiple_of(c * chunk, chunk), chunk)

    def rows(p):
        return pl.ds(pl.multiple_of(p * quarter, quarter), quarter)

    def loads(c):
        return [
            pltpu.make_async_copy(
                src.at[0, :, cols(c)], own.at[a, :, cols(c)], load_sem.at[c, a]
            )
            for a, src in ((K, k_hbm), (V, v_hbm), (Q, q_hbm))
        ]

    def swaps(c):
        copies = []
        for d in range(1, TEAM):
            peer = lax.rem(place + d, TEAM)
            copies.append(
                pltpu.make_async_remote_copy(
                    src_ref=own.at[:, rows(peer), cols(c)],
                    dst_ref=swap.at[place + REACH, :, :, cols(c)],
                    send_sem=swap_send.at[c, d - 1],
                    recv_sem=swap_recv.at[c, d - 1],
                    device_id={"queue": team + peer},
                    device_id_type=pl.DeviceIdType.MESH,
                )
            )
        return copies

    def swap_own(c):
        return pltpu.make_async_copy(
            own.at[:, rows(place), cols(c)],
            swap.at[place + REACH, :, :, cols(c)],
            swap_local.at[c],
        )

    def halos(c):
        copies = []
        for way, src, dst, target in (
            (0, TEAM, 0, following),
            (1, REACH, TEAM + REACH, previous),
        ):
            copies.append(
                pltpu.make_async_remote_copy(
                    src_ref=swap.at[pl.ds(src, REACH), pl.ds(0, 2), :, cols(c)],
                    dst_ref=swap.at[pl.ds(dst, REACH), pl.ds(0, 2), :, cols(c)],
                    send_sem=halo_send.at[c, way],
                    recv_sem=halo_recv.at[c, way],
                    device_id={"queue": target},
                    device_id_type=pl.DeviceIdType.MESH,
                )
            )
        return copies

    def result_at(j):
        return j + TEAM * (j // 2)

    def backs(c):
        copies = []
        for d in range(1, TEAM):
            peer = lax.rem(place + d, TEAM)
            copies.append(
                pltpu.make_async_remote_copy(
                    src_ref=swap.at[result_at(peer), Q, :, cols(c)],
                    dst_ref=back.at[rows(place), cols(c)],
                    send_sem=back_send.at[c, d - 1],
                    recv_sem=back_recv.at[c, d - 1],
                    device_id={"queue": team + peer},
                    device_id_type=pl.DeviceIdType.MESH,
                )
            )
        return copies

    def back_own(c):
        return pltpu.make_async_copy(
            swap.at[result_at(place), Q, :, cols(c)],
            back.at[rows(place), cols(c)],
            back_local.at[c],
        )

    def store_out(c):
        return pltpu.make_async_copy(
            back.at[:, cols(c)], out_hbm.at[0, :, cols(c)], out_sem.at[c]
        )

    def start_load(c, _):
        for copy in loads(c):
            copy.start()
        return 0

    def start_swap(c):
        for copy in loads(c):
            copy.wait()
        for copy in swaps(c):
            copy.start()
        swap_own(c).start()

    def head_cols(c, h):
        return pl.ds(pl.multiple_of(c * chunk + h * HEAD_DIM, HEAD_DIM), HEAD_DIM)

    level = levels_ref[slot]

    def do_spatial(c):
        for h in range(CHUNK_HEADS):
            hc = head_cols(c, h)
            keys = own[K, :, hc]
            vals = own[V, :, hc]
            vals = jnp.concatenate([vals, jnp.ones_like(vals)], axis=1)
            gate = gate_ref[level, 0:1, hc]
            for r in range(0, tokens, ROW_BLOCK):
                rs = pl.ds(r, ROW_BLOCK)
                s = lax.dot_general(
                    own[Q, rs, hc],
                    keys,
                    (((1,), (1,)), ((), ())),
                    preferred_element_type=jnp.float32,
                )
                top = jnp.max(s, axis=1, keepdims=True)
                e = jnp.exp2((s - top) * coef).astype(jnp.bfloat16)
                o = jnp.dot(e, vals, preferred_element_type=jnp.float32)
                spatial[rs, hc] = gate * (o[:, :HEAD_DIM] / o[:, HEAD_DIM:])

    def do_temporal(c):
        ones = jnp.ones((2 * HEAD_DIM, HEAD_DIM), jnp.bfloat16)

        def one_slot(j, _):
            at = team + j
            position = lax.rem(at - head_ref[0] + n, n)
            reach = window_ref[at]
            for h in range(CHUNK_HEADS):
                hc = head_cols(c, h)
                query = swap[j + REACH, Q, :, hc].astype(jnp.float32)
                scores = []
                for o in range(2 * REACH + 1):
                    offset = o - REACH
                    product = query * swap[j + o, K, :, hc].astype(jnp.float32)
                    high = product.astype(jnp.bfloat16)
                    low = (product - high.astype(jnp.float32)).astype(jnp.bfloat16)
                    s = (
                        jnp.dot(
                            jnp.concatenate([high, low], axis=1),
                            ones,
                            preferred_element_type=jnp.float32,
                        )
                        * coef
                    )
                    if offset:
                        valid = (
                            (reach >= abs(offset))
                            & (position + offset >= 0)
                            & (position + offset < n)
                        )
                        s = s + jnp.where(valid, 0.0, -1e30).astype(jnp.float32)
                    scores.append(s)
                top = functools.reduce(jnp.maximum, scores)
                total = 0.0
                mixed = 0.0
                for o in range(2 * REACH + 1):
                    e = jnp.exp2(scores[o] - top)
                    total = total + e
                    mixed = mixed + e * swap[j + o, V, :, hc].astype(jnp.float32)
                swap[result_at(j), Q, :, hc] = (mixed / total).astype(jnp.bfloat16)
            return 0

        lax.fori_loop(0, TEAM, one_slot, 0)

    def do_blend(c):
        for h in range(CHUNK_HEADS):
            hc = head_cols(c, h)
            gate = gate_ref[level, 1:2, hc]
            mixed = spatial[:, hc] + gate * back[:, hc].astype(jnp.float32)
            back[:, hc] = mixed.astype(jnp.bfloat16)

    lax.fori_loop(0, count, start_load, 0)
    barrier = pltpu.get_barrier_semaphore()
    mates = [team + lax.rem(place + d, TEAM) for d in range(1, TEAM)]
    for other in mates + [following, previous]:
        pl.semaphore_signal(
            barrier, inc=1, device_id={"queue": other}, device_id_type=pl.DeviceIdType.MESH
        )
    pl.semaphore_wait(barrier, TEAM + 1)

    def first(c, _):
        start_swap(c)
        return 0

    lax.fori_loop(0, AHEAD, first, 0)

    def step(i, _):
        @pl.when(i < count)
        def _():
            for copy in swaps(i):
                copy.wait_recv()
            swap_own(i).wait()
            for copy in halos(i):
                copy.start()

            @pl.when(i + AHEAD < count)
            def _():
                start_swap(i + AHEAD)

            do_spatial(i)

        t = i - LAG_TEMPORAL

        @pl.when((t >= 0) & (t < count))
        def _():
            for copy in halos(t):
                copy.wait_recv()
            do_temporal(t)
            for copy in backs(t):
                copy.start()
            back_own(t).start()

        b = t - LAG_BLEND

        @pl.when(b >= 0)
        def _():
            for copy in backs(b):
                copy.wait_recv()
            back_own(b).wait()
            do_blend(b)
            store_out(b).start()

        return 0

    lax.fori_loop(0, count + LAG_TEMPORAL + LAG_BLEND, step, 0)

    def finish(c, _):
        for copy in swaps(c) + halos(c) + backs(c):
            copy.wait_send()
        store_out(c).wait()
        return 0

    lax.fori_loop(0, count, finish, 0)


def body(query, keys, values, gate_table, levels, window, queue_head):
    n = lax.axis_size("queue")
    _, tokens, width = query.shape
    count = width // (CHUNK_HEADS * HEAD_DIM)
    dma = pltpu.SemaphoreType.DMA
    smem = pl.BlockSpec(memory_space=pltpu.SMEM)
    hbm = pl.BlockSpec(memory_space=pl.ANY)
    return pl.pallas_call(
        functools.partial(kernel, n),
        out_shape=jax.ShapeDtypeStruct(query.shape, jnp.bfloat16),
        in_specs=[smem, smem, smem, pl.BlockSpec(memory_space=pltpu.VMEM), hbm, hbm, hbm],
        out_specs=hbm,
        scratch_shapes=[
            pltpu.VMEM((3, tokens, width), jnp.bfloat16),
            pltpu.VMEM((TEAM + 2 * REACH, 3, tokens // TEAM, width), jnp.bfloat16),
            pltpu.VMEM((tokens, width), jnp.float32),
            pltpu.VMEM((tokens, width), jnp.bfloat16),
            dma((count, 3)),
            dma((count, TEAM - 1)),
            dma((count, TEAM - 1)),
            dma((count,)),
            dma((count, 2)),
            dma((count, 2)),
            dma((count, TEAM - 1)),
            dma((count, TEAM - 1)),
            dma((count,)),
            dma((count,)),
        ],
        compiler_params=pltpu.CompilerParams(
            collective_id=0, has_side_effects=True, vmem_limit_bytes=60 * 2**20
        ),
        cost_estimate=pl.CostEstimate(
            flops=4 * tokens * tokens * width,
            bytes_accessed=8 * tokens * width,
            transcendentals=tokens * tokens * width // HEAD_DIM,
        ),
    )(levels, window, queue_head, gate_table, query, keys, values)


def solution(mesh):
    spread = P(("groups", "queue"), None, None)
    in_specs = (spread, spread, spread, P(), P("groups"), P("groups"), P("groups"))
    return jax.shard_map(body, mesh=mesh, in_specs=in_specs, out_specs=spread, check_vma=False)
```

```python
import functools
import math

import jax
import jax.numpy as jnp
from jax import lax
from jax.experimental import pallas as pl
from jax.experimental.pallas import tpu as pltpu
from jax.sharding import PartitionSpec as P

HEAD_DIM = 128
REACH = 2
TEAM = 4
CHUNK_HEADS = 1
ROW_BLOCK = 256
AHEAD = 2
LAG_TEMPORAL = 1
LAG_BLEND = 1
K, V, Q = 0, 1, 2


def kernel(
    n,
    levels_ref,
    window_ref,
    head_ref,
    gate_hbm,
    q_hbm,
    k_hbm,
    v_hbm,
    out_hbm,
    own,
    swap,
    spatial,
    gate_ref,
    back,
    gate_sem,
    load_sem,
    swap_send,
    swap_recv,
    swap_local,
    direct_send,
    direct_recv,
    halo_send,
    halo_recv,
    back_send,
    back_recv,
    back_local,
    out_sem,
):
    tokens, width = back.shape
    quarter = tokens // TEAM
    chunk = CHUNK_HEADS * HEAD_DIM
    count = width // chunk
    coef = math.log2(math.e) / math.sqrt(HEAD_DIM)

    slot = lax.axis_index("queue")
    place = lax.rem(slot, TEAM)
    team = slot - place
    half = place // REACH
    core = lax.rem(place, REACH)

    def cols(c):
        return pl.ds(pl.multiple_of(c * chunk, chunk), chunk)

    def rows(p):
        return pl.ds(pl.multiple_of(p * quarter, quarter), quarter)

    def loads(c):
        return [
            pltpu.make_async_copy(
                src.at[0, :, cols(c)], own.at[a, :, cols(c)], load_sem.at[c, a]
            )
            for a, src in ((K, k_hbm), (V, v_hbm), (Q, q_hbm))
        ]

    def swaps(c, part):
        arrays = pl.ds(0, 2) if part == 0 else pl.ds(Q, 1)
        copies = []
        for d in range(1, TEAM):
            peer = lax.rem(place + d, TEAM)
            copies.append(
                pltpu.make_async_remote_copy(
                    src_ref=own.at[arrays, rows(peer), cols(c)],
                    dst_ref=swap.at[place + REACH, arrays, :, cols(c)],
                    send_sem=swap_send.at[c, part, d - 1],
                    recv_sem=swap_recv.at[c, part, d - 1],
                    device_id={"queue": team + peer},
                    device_id_type=pl.DeviceIdType.MESH,
                )
            )
        return copies

    def swap_own(c):
        return pltpu.make_async_copy(
            own.at[:, rows(place), cols(c)],
            swap.at[place + REACH, :, :, cols(c)],
            swap_local.at[c],
        )

    def direct(c, target, source):
        return pltpu.make_async_remote_copy(
            src_ref=own.at[pl.ds(0, 2), rows(REACH * half + target), cols(c)],
            dst_ref=swap.at[TEAM + REACH + source - 6 * half, pl.ds(0, 2), :, cols(c)],
            send_sem=direct_send.at[c, target],
            recv_sem=direct_recv.at[c, source],
            device_id={"queue": lax.rem(slot - core + target + n + TEAM * (2 * half - 1), n)},
            device_id_type=pl.DeviceIdType.MESH,
        )

    def halo(c):
        return pltpu.make_async_remote_copy(
            src_ref=swap.at[pl.ds(TEAM - REACH * half, REACH), pl.ds(0, 2), :, cols(c)],
            dst_ref=swap.at[pl.ds(6 * half, REACH), pl.ds(0, 2), :, cols(c)],
            send_sem=halo_send.at[c],
            recv_sem=halo_recv.at[c],
            device_id={"queue": lax.rem(slot + n + TEAM * (1 - 2 * half), n)},
            device_id_type=pl.DeviceIdType.MESH,
        )

    def result_at(j):
        return j + TEAM * (j // 2)

    def backs(c):
        copies = []
        for d in range(1, TEAM):
            peer = lax.rem(place + d, TEAM)
            copies.append(
                pltpu.make_async_remote_copy(
                    src_ref=swap.at[result_at(peer), Q, :, cols(c)],
                    dst_ref=back.at[rows(place), cols(c)],
                    send_sem=back_send.at[c, d - 1],
                    recv_sem=back_recv.at[c, d - 1],
                    device_id={"queue": team + peer},
                    device_id_type=pl.DeviceIdType.MESH,
                )
            )
        return copies

    def back_own(c):
        return pltpu.make_async_copy(
            swap.at[result_at(place), Q, :, cols(c)],
            back.at[rows(place), cols(c)],
            back_local.at[c],
        )

    def store_out(c):
        return pltpu.make_async_copy(
            back.at[:, cols(c)], out_hbm.at[0, :, cols(c)], out_sem.at[c]
        )

    def start_load(c, _):
        for copy in loads(c):
            copy.start()
        return 0

    def start_swap(c):
        for copy in loads(c):
            copy.wait()
        for copy in swaps(c, 0):
            copy.start()
        for e in range(REACH):
            direct(c, e, core).start()
        swap_own(c).start()

    def start_queries(c):
        for copy in swaps(c, 1):
            copy.start()

    def head_cols(c, h):
        return pl.ds(pl.multiple_of(c * chunk + h * HEAD_DIM, HEAD_DIM), HEAD_DIM)

    level = levels_ref[slot]

    def do_spatial(c):
        for h in range(CHUNK_HEADS):
            hc = head_cols(c, h)
            keys = own[K, :, hc]
            vals = own[V, :, hc]
            vals = jnp.concatenate([vals, jnp.ones_like(vals)], axis=1)
            gate = gate_ref[level, 0:1, hc]
            for r in range(0, tokens, ROW_BLOCK):
                rs = pl.ds(r, ROW_BLOCK)
                s = lax.dot_general(
                    own[Q, rs, hc],
                    keys,
                    (((1,), (1,)), ((), ())),
                    preferred_element_type=jnp.float32,
                )
                top = jnp.max(s, axis=1, keepdims=True)
                e = jnp.exp2((s - top) * coef).astype(jnp.bfloat16)
                o = jnp.dot(e, vals, preferred_element_type=jnp.float32)
                spatial[rs, hc] = gate * (o[:, :HEAD_DIM] / o[:, HEAD_DIM:])

    def do_temporal(c):
        ones = jnp.ones((2 * HEAD_DIM, HEAD_DIM), jnp.bfloat16)

        def one_slot(j, _):
            at = team + j
            position = lax.rem(at - head_ref[0] + n, n)
            reach = window_ref[at]
            for h in range(CHUNK_HEADS):
                hc = head_cols(c, h)
                query = swap[j + REACH, Q, :, hc].astype(jnp.float32)
                scores = []
                for o in range(2 * REACH + 1):
                    offset = o - REACH
                    product = query * swap[j + o, K, :, hc].astype(jnp.float32)
                    high = product.astype(jnp.bfloat16)
                    low = (product - high.astype(jnp.float32)).astype(jnp.bfloat16)
                    s = (
                        jnp.dot(
                            jnp.concatenate([high, low], axis=1),
                            ones,
                            preferred_element_type=jnp.float32,
                        )
                        * coef
                    )
                    if offset:
                        valid = (
                            (reach >= abs(offset))
                            & (position + offset >= 0)
                            & (position + offset < n)
                        )
                        s = s + jnp.where(valid, 0.0, -1e30).astype(jnp.float32)
                    scores.append(s)
                top = functools.reduce(jnp.maximum, scores)
                total = 0.0
                mixed = 0.0
                for o in range(2 * REACH + 1):
                    e = jnp.exp2(scores[o] - top)
                    total = total + e
                    mixed = mixed + e * swap[j + o, V, :, hc].astype(jnp.float32)
                swap[result_at(j), Q, :, hc] = (mixed / total).astype(jnp.bfloat16)
            return 0

        lax.fori_loop(0, TEAM, one_slot, 0)

    def do_blend(c):
        for h in range(CHUNK_HEADS):
            hc = head_cols(c, h)
            gate = gate_ref[level, 1:2, hc]
            mixed = spatial[:, hc] + gate * back[:, hc].astype(jnp.float32)
            back[:, hc] = mixed.astype(jnp.bfloat16)

    lax.fori_loop(0, AHEAD, start_load, 0)
    gates = pltpu.make_async_copy(gate_hbm, gate_ref, gate_sem)
    barrier = pltpu.get_barrier_semaphore()
    others = [team + lax.rem(place + d, TEAM) for d in range(1, TEAM)]
    for e in range(REACH):
        others.append(lax.rem(slot - core + e + TEAM, n))
        others.append(lax.rem(slot - core + e + n - TEAM, n))
    for other in others:
        pl.semaphore_signal(
            barrier, inc=1, device_id={"queue": other}, device_id_type=pl.DeviceIdType.MESH
        )
    pl.semaphore_wait(barrier, len(others))

    for c in range(AHEAD):
        start_swap(c)
    lax.fori_loop(AHEAD, count, start_load, 0)
    gates.start()
    for c in range(AHEAD - 1):
        start_queries(c)
    gates.wait()

    def step(i, _):
        @pl.when(i < count)
        def _():
            for copy in swaps(i, 0):
                copy.wait_recv()
            swap_own(i).wait()
            halo(i).start()

            @pl.when(i + AHEAD < count)
            def _():
                start_swap(i + AHEAD)

            @pl.when(i + AHEAD - 1 < count)
            def _():
                start_queries(i + AHEAD - 1)

            do_spatial(i)

        t = i - LAG_TEMPORAL

        @pl.when((t >= 0) & (t < count))
        def _():
            for copy in swaps(t, 1):
                copy.wait_recv()
            for e in range(REACH):
                direct(t, e, e).wait_recv()
            halo(t).wait_recv()
            do_temporal(t)
            for copy in backs(t):
                copy.start()
            back_own(t).start()

        b = t - LAG_BLEND

        @pl.when(b >= 0)
        def _():
            for copy in backs(b):
                copy.wait_recv()
            back_own(b).wait()
            do_blend(b)
            store_out(b).start()

        return 0

    lax.fori_loop(0, count + LAG_TEMPORAL + LAG_BLEND, step, 0)

    def finish(c, _):
        for copy in swaps(c, 0) + swaps(c, 1) + backs(c) + [halo(c)]:
            copy.wait_send()
        for e in range(REACH):
            direct(c, e, core).wait_send()
        store_out(c).wait()
        return 0

    lax.fori_loop(0, count, finish, 0)


def body(query, keys, values, gate_table, levels, window, queue_head):
    n = lax.axis_size("queue")
    _, tokens, width = query.shape
    count = width // (CHUNK_HEADS * HEAD_DIM)
    dma = pltpu.SemaphoreType.DMA
    smem = pl.BlockSpec(memory_space=pltpu.SMEM)
    hbm = pl.BlockSpec(memory_space=pl.ANY)
    return pl.pallas_call(
        functools.partial(kernel, n),
        out_shape=jax.ShapeDtypeStruct(query.shape, jnp.bfloat16),
        in_specs=[smem, smem, smem, hbm, hbm, hbm, hbm],
        out_specs=hbm,
        scratch_shapes=[
            pltpu.VMEM((3, tokens, width), jnp.bfloat16),
            pltpu.VMEM((TEAM + 2 * REACH, 3, tokens // TEAM, width), jnp.bfloat16),
            pltpu.VMEM((tokens, width), jnp.float32),
            pltpu.VMEM(gate_table.shape, jnp.float32),
            pltpu.VMEM((tokens, width), jnp.bfloat16),
            dma,
            dma((count, 3)),
            dma((count, 2, TEAM - 1)),
            dma((count, 2, TEAM - 1)),
            dma((count,)),
            dma((count, 2)),
            dma((count, 2)),
            dma((count,)),
            dma((count,)),
            dma((count, TEAM - 1)),
            dma((count, TEAM - 1)),
            dma((count,)),
            dma((count,)),
        ],
        compiler_params=pltpu.CompilerParams(
            collective_id=0, has_side_effects=True, vmem_limit_bytes=60 * 2**20
        ),
        cost_estimate=pl.CostEstimate(
            flops=4 * tokens * tokens * width,
            bytes_accessed=8 * tokens * width,
            transcendentals=tokens * tokens * width // HEAD_DIM,
        ),
    )(levels, window, queue_head, gate_table, query, keys, values)


def solution(mesh):
    spread = P(("groups", "queue"), None, None)
    in_specs = (spread, spread, spread, P(), P("groups"), P("groups"), P("groups"))
    return jax.shard_map(body, mesh=mesh, in_specs=in_specs, out_specs=spread, check_vma=False)
```

```python
import functools
import math

import jax
import jax.numpy as jnp
from jax import lax
from jax.experimental import pallas as pl
from jax.experimental.pallas import tpu as pltpu
from jax.sharding import PartitionSpec as P

HEAD_DIM = 128
REACH = 2
TEAM = 4
CHUNK_HEADS = 1
ROW_BLOCK = 256
AHEAD = 2
LAG_TEMPORAL = 1
LAG_BLEND = 1
K, V, Q = 0, 1, 2


def kernel(
    n,
    levels_ref,
    window_ref,
    head_ref,
    gate_hbm,
    q_hbm,
    k_hbm,
    v_hbm,
    out_hbm,
    own,
    swap,
    spatial,
    gate_ref,
    back,
    gate_sem,
    load_sem,
    swap_send,
    swap_recv,
    swap_local,
    direct_send,
    direct_recv,
    halo_send,
    halo_recv,
    back_send,
    back_recv,
    back_local,
    out_sem,
):
    tokens, width = back.shape
    quarter = tokens // TEAM
    chunk = CHUNK_HEADS * HEAD_DIM
    count = width // chunk
    coef = math.log2(math.e) / math.sqrt(HEAD_DIM)

    slot = lax.axis_index("queue")
    place = lax.rem(slot, TEAM)
    team = slot - place
    half = place // REACH
    core = lax.rem(place, REACH)

    def cols(c):
        return pl.ds(pl.multiple_of(c * chunk, chunk), chunk)

    def rows(p):
        return pl.ds(pl.multiple_of(p * quarter, quarter), quarter)

    def loads(c):
        return [
            pltpu.make_async_copy(
                src.at[0, :, cols(c)], own.at[a, :, cols(c)], load_sem.at[c, a]
            )
            for a, src in ((K, k_hbm), (V, v_hbm), (Q, q_hbm))
        ]

    def swaps(c, part):
        arrays = pl.ds(0, 2) if part == 0 else pl.ds(Q, 1)
        copies = []
        for d in range(1, TEAM):
            peer = lax.rem(place + d, TEAM)
            copies.append(
                pltpu.make_async_remote_copy(
                    src_ref=own.at[arrays, rows(peer), cols(c)],
                    dst_ref=swap.at[place + REACH, arrays, :, cols(c)],
                    send_sem=swap_send.at[c, part, d - 1],
                    recv_sem=swap_recv.at[c, part, d - 1],
                    device_id={"queue": team + peer},
                    device_id_type=pl.DeviceIdType.MESH,
                )
            )
        return copies

    def swap_own(c):
        return pltpu.make_async_copy(
            own.at[:, rows(place), cols(c)],
            swap.at[place + REACH, :, :, cols(c)],
            swap_local.at[c],
        )

    def direct(c, target, source):
        return pltpu.make_async_remote_copy(
            src_ref=own.at[pl.ds(0, 2), rows(REACH * half + target), cols(c)],
            dst_ref=swap.at[TEAM + REACH + source - 6 * half, pl.ds(0, 2), :, cols(c)],
            send_sem=direct_send.at[c, target],
            recv_sem=direct_recv.at[c, source],
            device_id={"queue": lax.rem(slot - core + target + n + TEAM * (2 * half - 1), n)},
            device_id_type=pl.DeviceIdType.MESH,
        )

    def halo(c):
        return pltpu.make_async_remote_copy(
            src_ref=swap.at[pl.ds(TEAM - REACH * half, REACH), pl.ds(0, 2), :, cols(c)],
            dst_ref=swap.at[pl.ds(6 * half, REACH), pl.ds(0, 2), :, cols(c)],
            send_sem=halo_send.at[c],
            recv_sem=halo_recv.at[c],
            device_id={"queue": lax.rem(slot + n + TEAM * (1 - 2 * half), n)},
            device_id_type=pl.DeviceIdType.MESH,
        )

    def result_at(j):
        return j + TEAM * (j // 2)

    def backs(c):
        copies = []
        for d in range(1, TEAM):
            peer = lax.rem(place + d, TEAM)
            copies.append(
                pltpu.make_async_remote_copy(
                    src_ref=swap.at[result_at(peer), Q, :, cols(c)],
                    dst_ref=back.at[rows(place), cols(c)],
                    send_sem=back_send.at[c, d - 1],
                    recv_sem=back_recv.at[c, d - 1],
                    device_id={"queue": team + peer},
                    device_id_type=pl.DeviceIdType.MESH,
                )
            )
        return copies

    def back_own(c):
        return pltpu.make_async_copy(
            swap.at[result_at(place), Q, :, cols(c)],
            back.at[rows(place), cols(c)],
            back_local.at[c],
        )

    def store_out(c):
        return pltpu.make_async_copy(
            back.at[:, cols(c)], out_hbm.at[0, :, cols(c)], out_sem.at[c]
        )

    def start_load(c, _):
        for copy in loads(c):
            copy.start()
        return 0

    def start_swap(c):
        for copy in loads(c):
            copy.wait()
        for copy in swaps(c, 0):
            copy.start()
        for e in range(REACH):
            direct(c, e, core).start()
        swap_own(c).start()

    def start_queries(c):
        for copy in swaps(c, 1):
            copy.start()

    def head_cols(c, h):
        return pl.ds(pl.multiple_of(c * chunk + h * HEAD_DIM, HEAD_DIM), HEAD_DIM)

    level = levels_ref[slot]

    def do_spatial(c):
        for h in range(CHUNK_HEADS):
            hc = head_cols(c, h)
            keys = own[K, :, hc]
            vals = own[V, :, hc]
            vals = jnp.concatenate([vals, jnp.ones_like(vals)], axis=1)
            gate = gate_ref[level, 0:1, hc]
            for r in range(0, tokens, ROW_BLOCK):
                rs = pl.ds(r, ROW_BLOCK)
                s = lax.dot_general(
                    own[Q, rs, hc],
                    keys,
                    (((1,), (1,)), ((), ())),
                    preferred_element_type=jnp.float32,
                )
                top = jnp.max(s, axis=1, keepdims=True)
                e = jnp.exp2((s - top) * coef).astype(jnp.bfloat16)
                o = jnp.dot(e, vals, preferred_element_type=jnp.float32)
                spatial[rs, hc] = gate * (o[:, :HEAD_DIM] / o[:, HEAD_DIM:])

    def do_temporal(c):
        ones = jnp.ones((2 * HEAD_DIM, HEAD_DIM), jnp.bfloat16)

        def one_slot(j, _):
            at = team + j
            position = lax.rem(at - head_ref[0] + n, n)
            reach = window_ref[at]
            for h in range(CHUNK_HEADS):
                hc = head_cols(c, h)
                query = swap[j + REACH, Q, :, hc].astype(jnp.float32)
                scores = []
                for o in range(2 * REACH + 1):
                    offset = o - REACH
                    product = query * swap[j + o, K, :, hc].astype(jnp.float32)
                    high = product.astype(jnp.bfloat16)
                    low = (product - high.astype(jnp.float32)).astype(jnp.bfloat16)
                    s = (
                        jnp.dot(
                            jnp.concatenate([high, low], axis=1),
                            ones,
                            preferred_element_type=jnp.float32,
                        )
                        * coef
                    )
                    if offset:
                        valid = (
                            (reach >= abs(offset))
                            & (position + offset >= 0)
                            & (position + offset < n)
                        )
                        s = s + jnp.where(valid, 0.0, -1e30).astype(jnp.float32)
                    scores.append(s)
                top = functools.reduce(jnp.maximum, scores)
                total = 0.0
                mixed = 0.0
                for o in range(2 * REACH + 1):
                    e = jnp.exp2(scores[o] - top)
                    total = total + e
                    mixed = mixed + e * swap[j + o, V, :, hc].astype(jnp.float32)
                swap[result_at(j), Q, :, hc] = (mixed / total).astype(jnp.bfloat16)
            return 0

        lax.fori_loop(0, TEAM, one_slot, 0)

    def do_blend(c):
        for h in range(CHUNK_HEADS):
            hc = head_cols(c, h)
            gate = gate_ref[level, 1:2, hc]
            mixed = spatial[:, hc] + gate * back[:, hc].astype(jnp.float32)
            back[:, hc] = mixed.astype(jnp.bfloat16)

    lax.fori_loop(0, AHEAD, start_load, 0)
    gates = pltpu.make_async_copy(gate_hbm, gate_ref, gate_sem)
    barrier = pltpu.get_barrier_semaphore()
    others = [team + lax.rem(place + d, TEAM) for d in range(1, TEAM)]
    for e in range(REACH):
        others.append(lax.rem(slot - core + e + TEAM, n))
        others.append(lax.rem(slot - core + e + n - TEAM, n))
    for other in others:
        pl.semaphore_signal(
            barrier, inc=1, device_id={"queue": other}, device_id_type=pl.DeviceIdType.MESH
        )
    pl.semaphore_wait(barrier, len(others))

    for c in range(AHEAD):
        start_swap(c)
    lax.fori_loop(AHEAD, count, start_load, 0)
    gates.start()
    for c in range(AHEAD - 1):
        start_queries(c)
    gates.wait()

    def step(i, _):
        @pl.when(i < count)
        def _():
            for copy in swaps(i, 0):
                copy.wait_recv()
            swap_own(i).wait()
            halo(i).start()

            @pl.when(i + AHEAD < count)
            def _():
                start_swap(i + AHEAD)

            @pl.when(i + AHEAD - 1 < count)
            def _():
                start_queries(i + AHEAD - 1)

        t = i - LAG_TEMPORAL

        @pl.when((t >= 0) & (t < count))
        def _():
            for copy in swaps(t, 1):
                copy.wait_recv()
            for e in range(REACH):
                direct(t, e, e).wait_recv()
            halo(t).wait_recv()
            do_temporal(t)
            for copy in backs(t):
                copy.start()
            back_own(t).start()

        @pl.when(i < count)
        def _():
            do_spatial(i)

        b = t - LAG_BLEND

        @pl.when(b >= 0)
        def _():
            for copy in backs(b):
                copy.wait_recv()
            back_own(b).wait()
            do_blend(b)
            store_out(b).start()

        return 0

    lax.fori_loop(0, count + LAG_TEMPORAL + LAG_BLEND, step, 0)

    def finish(c, _):
        for copy in swaps(c, 0) + swaps(c, 1) + backs(c) + [halo(c)]:
            copy.wait_send()
        for e in range(REACH):
            direct(c, e, core).wait_send()
        store_out(c).wait()
        return 0

    lax.fori_loop(0, count, finish, 0)


def body(query, keys, values, gate_table, levels, window, queue_head):
    n = lax.axis_size("queue")
    _, tokens, width = query.shape
    count = width // (CHUNK_HEADS * HEAD_DIM)
    dma = pltpu.SemaphoreType.DMA
    smem = pl.BlockSpec(memory_space=pltpu.SMEM)
    hbm = pl.BlockSpec(memory_space=pl.ANY)
    return pl.pallas_call(
        functools.partial(kernel, n),
        out_shape=jax.ShapeDtypeStruct(query.shape, jnp.bfloat16),
        in_specs=[smem, smem, smem, hbm, hbm, hbm, hbm],
        out_specs=hbm,
        scratch_shapes=[
            pltpu.VMEM((3, tokens, width), jnp.bfloat16),
            pltpu.VMEM((TEAM + 2 * REACH, 3, tokens // TEAM, width), jnp.bfloat16),
            pltpu.VMEM((tokens, width), jnp.float32),
            pltpu.VMEM(gate_table.shape, jnp.float32),
            pltpu.VMEM((tokens, width), jnp.bfloat16),
            dma,
            dma((count, 3)),
            dma((count, 2, TEAM - 1)),
            dma((count, 2, TEAM - 1)),
            dma((count,)),
            dma((count, 2)),
            dma((count, 2)),
            dma((count,)),
            dma((count,)),
            dma((count, TEAM - 1)),
            dma((count, TEAM - 1)),
            dma((count,)),
            dma((count,)),
        ],
        compiler_params=pltpu.CompilerParams(
            collective_id=0, has_side_effects=True, vmem_limit_bytes=60 * 2**20
        ),
        cost_estimate=pl.CostEstimate(
            flops=4 * tokens * tokens * width,
            bytes_accessed=8 * tokens * width,
            transcendentals=tokens * tokens * width // HEAD_DIM,
        ),
    )(levels, window, queue_head, gate_table, query, keys, values)


def solution(mesh):
    spread = P(("groups", "queue"), None, None)
    in_specs = (spread, spread, spread, P(), P("groups"), P("groups"), P("groups"))
    return jax.shard_map(body, mesh=mesh, in_specs=in_specs, out_specs=spread, check_vma=False)
```
